512 devices in a mesh: seq: 16 (over x_hi, y), chan: 32 (over z, x_lo, core).
Axes of the slice: x: 4 (x_hi: 2, x_lo: 2; x = x_hi * 2 + x_lo), y: 8, z: 8, core: 2. Of those that a mesh axis runs over, the one named last changes fastest.
Arguments:
- query_gate: bfloat16 [8192, 8192], P('seq', 'chan'), may hold values from -6 to 6
- key_gate: bfloat16 [8192, 8192], P('seq', 'chan'), may hold values from -6 to 6
- values_in: bfloat16 [8192, 8192], P('seq', 'chan'), may hold values from -6 to 6
- cotangent: bfloat16 [8192, 8192], P('seq', 'chan'), may hold values from -6 to 6
- decay_rate: float32 [512, 16], P('chan'), may hold values from 3.6621094e-05 to 0.0333333333, as said below
- residues: float32 [512, 16], P('chan'), may hold values from -1.5 to 1.5
Outputs:
- mixed_out: bfloat16 [8192, 8192], P('seq', 'chan')
- query_grad: bfloat16 [8192, 8192], P('seq', 'chan')
- key_grad: bfloat16 [8192, 8192], P('seq', 'chan')
- value_grad: bfloat16 [8192, 8192], P('seq', 'chan')
- residue_grad: float32 [512, 16], P('chan')
The draws below stay inside these ranges and needn't reach their ends.
Inputs may be any that keep to these rules, and one draw needn't show every extreme that they name: `decay_rate`: positive decay rates.
All inputs are finite; a program needn't handle non-finite values.
Results may differ from the reference program's by a relative error of at most 0.005.
Values may be sent and summed in bfloat16 or wider, within the bound.
A program may use at most 64 MiB of HBM per device.

```python
import math
import jax
import jax.numpy as jnp
from jax import lax

C = 8192
GROUP = 16
M = 16
SEQ = 8192
G = 512


def draw_decay_rate(key, part):
    key = jax.random.fold_in(key, 7)
    pick_key, slow_key, fast_key = jax.random.split(key, 3)
    share = 0.5
    slow_log = jax.random.uniform(slow_key, (G, M), jnp.float32, math.log(0.3 / SEQ), math.log(2.0 / SEQ))
    fast_log = jax.random.uniform(fast_key, (G, M), jnp.float32, math.log(2.0 / SEQ), math.log(1.0 / 30.0))
    keeping = jax.random.uniform(pick_key, (G, M), jnp.float32) < share
    return jnp.exp(jnp.where(keeping, slow_log, fast_log))


def steps_of(rng, dims, cuts, low, top_value):
    gain, own = 1.0, jax.random.fold_in(rng, 6)
    for axis_at, shards_of in cuts:
        steps = jnp.exp(jax.random.uniform(jax.random.fold_in(own, axis_at), (shards_of,), jnp.float32, low / len(cuts), top_value / len(cuts)))
        gain = gain * jnp.repeat(steps, dims[axis_at] // shards_of).reshape([-1 if axis == axis_at else 1 for axis in range(len(dims))])
    return gain


def gaussian(own_key, shape, scale, limit, cuts=(), kind=jnp.bfloat16):
    array = jax.random.normal(own_key, shape, jnp.float32) * scale
    if len(cuts) > 0:
        array = steps_of(own_key, shape, cuts, -0.22, 0.18) * array
    return jnp.clip(array, min=-limit, max=limit).astype(kind)


def setup_inputs(seed: int = 0) -> dict:
    arg_keys = jax.random.split(jax.random.key(seed), 7)
    query_gate = gaussian(arg_keys[0], (SEQ, C), 1.0, 6.0, ((0, 16), (1, 32)))
    key_gate = gaussian(arg_keys[1], (SEQ, C), 1.0, 6.0, ((0, 16), (1, 32)))
    values_in = gaussian(arg_keys[2], (SEQ, C), 1.0, 6.0, ((0, 16), (1, 32)))
    cotangent = gaussian(arg_keys[3], (SEQ, C), 1.0, 6.0, ((0, 16), (1, 32)))
    decay_rate = draw_decay_rate(jax.random.fold_in(arg_keys[6], 71), 0)
    residues = gaussian(arg_keys[5], (G, M), M ** -0.5, 1.5, ((0, 32),), jnp.float32)
    return {"query_gate": query_gate, "key_gate": key_gate, "values_in": values_in, "cotangent": cotangent, "decay_rate": decay_rate, "residues": residues}


def expand_modes(mode_table):
    return jnp.repeat(mode_table.T, GROUP, axis=1)

def reference(query_gate, key_gate, values_in, cotangent, decay_rate, residues):
    factor = jnp.sqrt(1.0 - jnp.exp(-2.0 * decay_rate))
    scaled_cols = expand_modes(residues * factor)
    decay_cols = expand_modes(jnp.exp(-decay_rate))
    query_f = query_gate.astype(jnp.float32)
    cot_f = cotangent.astype(jnp.float32)
    gated_low = (key_gate.astype(jnp.float32) * values_in.astype(jnp.float32)).astype(jnp.bfloat16)
    gated_in = lax.optimization_barrier(gated_low).astype(jnp.float32)
    slope_grad = cot_f * query_f

    def forward_step(carry, inputs_now):
        state_now, accum = carry
        gated_now, slope_now = inputs_now
        state_now = decay_cols * state_now + gated_now[None, :]
        accum = accum + slope_now[None, :] * state_now
        return ((state_now, accum), lax.optimization_barrier(jnp.sum(scaled_cols * state_now, axis=0)))
    empty = jnp.zeros((M, C), jnp.float32)
    (state_end, accum), convolved = lax.scan(forward_step, (empty, empty), (gated_in, slope_grad))

    def back_step(state_now, slope_now):
        state_now = decay_cols * state_now + slope_now[None, :]
        return (state_now, lax.optimization_barrier(jnp.sum(scaled_cols * state_now, axis=0)))
    state_top, gated_grad = lax.scan(back_step, empty, slope_grad, reverse=True)
    residue_grad = lax.optimization_barrier(jnp.sum(accum.reshape(M, G, GROUP), axis=2)).T * factor
    mixed_out = (query_f * convolved).astype(jnp.bfloat16)
    query_grad = (cot_f * convolved).astype(jnp.bfloat16)
    key_grad = (gated_grad * values_in.astype(jnp.float32)).astype(jnp.bfloat16)
    value_grad = (gated_grad * key_gate.astype(jnp.float32)).astype(jnp.bfloat16)
    return (mixed_out, query_grad, key_grad, value_grad, residue_grad)
```

```python
import jax
import jax.numpy as jnp
from jax import lax
from jax.experimental import pallas as pl
from jax.experimental.pallas import tpu as pltpu
from jax.sharding import PartitionSpec as P

MESH = pl.DeviceIdType.MESH
f32 = jnp.float32
bf16 = jnp.bfloat16
GROUP = 16
MODES = 16
L = 64
QUARTER = 64
HIGH = lax.Precision.HIGHEST


def dot(a, b, dims=((1,), (0,)), precision=None):
    return lax.dot_general(
        a, b, (dims, ((), ())), precision=precision, preferred_element_type=f32
    )


def split(x):
    hi = x.astype(bf16)
    return hi, (x - hi.astype(f32)).astype(bf16)


def iota(shape, axis):
    return lax.broadcasted_iota(jnp.int32, shape, axis)


def pick_rows(m, rows):
    left = iota((rows, 128), 1) < QUARTER
    return jnp.concatenate(
        [
            jnp.where(left, m[:rows, :128], m[rows : 2 * rows, :128]),
            jnp.where(left, m[2 * rows : 3 * rows, 128:], m[3 * rows :, 128:]),
        ],
        axis=1,
    )


def kernel(
    peers,
    q_hbm, k_hbm, v_hbm, c_hbm, rate_hbm, res_hbm,
    mixed_ref, qgrad_ref, kgrad_ref, vgrad_ref, rgrad_ref,
    rate_ref, res_ref, q_s, k_s, v_s, c_s, x_s, sh_s, sl_s, conv_s, grad_s, fwd_s, bwd_s, bend_s,
    box, wbox, in_sem, send_sem, recv_sem,
):
    length = q_s.shape[0]
    width = q_s.shape[1]
    chunks = length // L
    me = lax.axis_index("seq")
    n = lax.axis_size("seq")
    loads = [
        pltpu.make_async_copy(src, dst, in_sem.at[i])
        for i, (src, dst) in enumerate(
            (
                (rate_hbm, rate_ref), (res_hbm, res_ref),
                (k_hbm, k_s), (v_hbm, v_s), (c_hbm, c_s), (q_hbm, q_s),
            )
        )
    ]
    for copy in loads:
        copy.start()
    ids = [peers(me, i) for i in range(n - 1)]
    barrier = pltpu.get_barrier_semaphore()
    for peer in ids:
        pl.semaphore_signal(barrier, inc=1, device_id={"seq": peer}, device_id_type=MESH)

    loads[0].wait()
    loads[1].wait()
    rate = rate_ref[...]
    factor = jnp.sqrt(1.0 - jnp.exp(-2.0 * rate))
    scaled = res_ref[...] * factor
    lane_hi = iota((16, width), 1) // GROUP
    lane_lo = iota((16, width), 1) % GROUP
    row16 = iota((16, width), 0)
    in_group = (lane_hi == row16).astype(f32)
    in_mode = (lane_lo == row16).astype(f32)
    rate_mc = dot(rate, in_group, ((0,), (0,)), HIGH)

    def row_of(x):
        return jnp.sum(dot(x, in_mode, precision=HIGH) * in_group, axis=0, keepdims=True)

    rate_row, scaled_row, factor_row = row_of(rate), row_of(scaled), row_of(factor)

    lane = iota((16, width), 1)
    position = (lane % L).astype(f32)
    end_parts = []
    start_parts = []
    for quarter in range(4):
        spread = (row16 == quarter * 4 + lane // L).astype(f32)
        rates = dot(rate, spread, ((0,), (0,)), HIGH)
        end_parts.append(jnp.exp((position - (L - 1.0)) * rates))
        start_parts.append(jnp.exp(-position * rates))
    end_hi, end_lo = zip(*[split(x) for x in end_parts])
    start_hi, start_lo = zip(*[split(x) for x in start_parts])

    def halves(hi, lo):
        return [
            jnp.concatenate([hi[2 * h], hi[2 * h + 1], lo[2 * h], lo[2 * h + 1]], axis=0)
            for h in range(2)
        ]

    end_pow = halves(end_hi, end_lo)
    start_pow = halves(start_hi, start_lo)

    lane64 = iota((L, width), 1)
    mask_i = [((lane64 // GROUP) % 4 == i).astype(bf16) for i in range(4)]
    mask_q = [(lane64 // QUARTER == q).astype(bf16) for q in range(4)]

    def spread_i(x):
        return jnp.concatenate([x * m for m in mask_i], axis=0)

    left16 = iota((16, 128), 1) < QUARTER

    def state_of(tables, pieces):
        out = []
        for h in range(2):
            first, *rest = pieces
            r = dot(tables[h], first[:, 128 * h : 128 * h + 128])
            r = r[:32] + r[32:]
            for piece in rest:
                r = r + dot(tables[h][:32], piece[:, 128 * h : 128 * h + 128])
            out.append(jnp.where(left16, r[:16], r[16:]))
        return jnp.concatenate(out, axis=1)

    decay_chunk = jnp.exp(-float(L) * rate_mc)
    decay_len = jnp.exp(-float(length) * rate_mc)
    decay_one = jnp.exp(-rate_mc)

    loads[2].wait()
    loads[3].wait()
    state = jnp.zeros((16, width), f32)
    for j in range(chunks):
        rows = pl.ds(j * L, L)
        x = (k_s[rows, :].astype(f32) * v_s[rows, :].astype(f32)).astype(bf16)
        x_s[rows, :] = x
        fwd_s[j] = state
        state = state * decay_chunk + state_of(end_pow, [spread_i(x)])
    end_state = state.astype(bf16)

    loads[4].wait()
    loads[5].wait()
    state = jnp.zeros((16, width), f32)
    for j in reversed(range(chunks)):
        rows = pl.ds(j * L, L)
        hi, lo = split(c_s[rows, :].astype(f32) * q_s[rows, :].astype(f32))
        sh_s[rows, :] = hi
        sl_s[rows, :] = lo
        bwd_s[j] = state
        here = state_of(start_pow, [spread_i(hi), spread_i(lo)])
        bend_s[j] = here
        state = state * decay_chunk + here
    box[0, me] = state.astype(bf16)
    box[1, me] = end_state

    pl.semaphore_wait(barrier, n - 1)
    sends = []
    for batch in range(2):
        for peer in ids:
            later = (peer > me).astype(jnp.int32)
            half = later if batch == 0 else 1 - later
            copy = pltpu.make_async_remote_copy(
                src_ref=box.at[half, me],
                dst_ref=box.at[batch, me],
                send_sem=send_sem.at[batch, peer],
                recv_sem=recv_sem.at[batch, me],
                device_id={"seq": peer},
                device_id_type=MESH,
            )
            copy.start()
            sends.append(copy)

    step = iota((L, width), 0).astype(f32)
    fall = jnp.exp(-step * rate_row)
    rise = jnp.exp(step * rate_row)
    q_of = iota((L, width), 1) // QUARTER
    fall_q = [jnp.where(q_of == q, fall, 0.0) for q in range(4)]
    rise_q = [jnp.where(q_of == q, rise, 0.0) for q in range(4)]
    fall_rows = jnp.concatenate(fall_q, axis=0)
    rise_rows = jnp.concatenate(rise_q, axis=0)

    def column(x):
        wide = dot(in_group, x, ((0,), (0,)), HIGH)
        keep = iota((width, MODES), 0) % MODES == iota((width, MODES), 1)
        ones = jnp.ones((MODES, width), f32)
        return dot(jnp.where(keep, wide, 0.0), ones, precision=HIGH)

    rate_col, scaled_col = column(rate), column(scaled)
    wide_lane = iota((width, width), 1)
    wide_row = iota((width, width), 0)
    same_i = (wide_row // MODES) % 4 == wide_lane // L
    at = (wide_lane % L).astype(f32)
    rise_cols = jnp.where(same_i, jnp.exp(at * rate_col), 0.0)
    fall_cols = jnp.where(same_i, scaled_col * jnp.exp(-at * rate_col), 0.0)

    def product(a, b):
        a_hi, a_lo = split(a)
        b_hi, b_lo = split(b)
        return dot(a_hi, b_hi) + (dot(a_lo, b_hi) + dot(a_hi, b_lo))

    row_at = wide_row % L
    col_at = wide_lane % L
    causal = row_at >= col_at
    filt = jnp.where(causal, product(fall_rows * scaled_row, rise_cols), 0.0).astype(bf16)
    anti = jnp.where(row_at <= col_at, product(rise_rows, fall_cols), 0.0).astype(bf16)

    gram = jnp.zeros((width, width), f32)
    cross = jnp.zeros((16, width), f32)
    for j in range(chunks):
        rows = pl.ds(j * L, L)
        hi = sh_s[rows, :]
        lhs = jnp.concatenate([hi * m for m in mask_q], axis=0)
        gram = gram + dot(lhs, spread_i(x_s[rows, :]), ((1,), (1,)))
        cross = cross + fwd_s[j] * bend_s[j]
    gram = jnp.where(causal, gram, 0.0)
    g_hi, g_lo = split(gram)
    r_hi = rise_cols.astype(bf16)
    within = dot(g_hi, r_hi, ((1,), (1,))) + dot(g_lo, r_hi, ((1,), (1,)))
    within = jnp.sum(within * fall_rows, axis=0, keepdims=True)
    same_group = ((wide_row // GROUP) == (wide_lane // GROUP)).astype(bf16)

    def group_row(z):
        hi, rest = z.astype(bf16), z - z.astype(bf16).astype(f32)
        mid, low = split(rest)
        s = dot(jnp.concatenate([hi, mid, low], axis=0), same_group)
        s = s[:16] + s[16:32] + s[32:]
        return jnp.sum(s * in_mode, axis=0, keepdims=True)

    wbox[me] = within + group_row(cross * decay_one)
    for peer in ids:
        copy = pltpu.make_async_remote_copy(
            src_ref=wbox.at[me],
            dst_ref=wbox.at[me],
            send_sem=send_sem.at[2, peer],
            recv_sem=recv_sem.at[2, me],
            device_id={"seq": peer},
            device_id_type=MESH,
        )
        copy.start()
        sends.append(copy)

    def block_rows(x):
        hi, lo = split(x)
        masks = [in_group[g : g + 1, :].astype(bf16) for g in range(16)]
        return (
            jnp.concatenate([hi * m for m in masks], axis=0),
            jnp.concatenate([lo * m for m in masks], axis=0),
        )

    def outer(table, blocks):
        t_hi, t_lo = table
        b_hi, b_lo = blocks
        return dot(t_hi, b_hi) + (dot(t_lo, b_hi) + dot(t_hi, b_lo))

    head = fall * jnp.exp(-rate_row) * scaled_row
    tail = rise * jnp.exp(-float(L) * rate_row) * scaled_row
    head_t, tail_t = split(head), split(tail)
    for j in range(chunks):
        rows = pl.ds(j * L, L)
        inner = pick_rows(dot(filt, spread_i(x_s[rows, :])), L)
        conv_s[rows, :] = inner + outer(head_t, block_rows(fwd_s[j]))
        inner = pick_rows(
            dot(anti, spread_i(sh_s[rows, :])) + dot(anti, spread_i(sl_s[rows, :])), L
        )
        grad_s[rows, :] = inner + outer(tail_t, block_rows(bwd_s[j]))

    def arrived(batch, peer):
        return pltpu.make_async_remote_copy(
            src_ref=box.at[batch, peer],
            dst_ref=box.at[batch, peer],
            send_sem=send_sem.at[batch, peer],
            recv_sem=recv_sem.at[batch, peer],
            device_id={"seq": peer},
            device_id_type=MESH,
        )

    for peer in ids:
        arrived(0, peer).wait_recv()
    entry_f = jnp.zeros((16, width), f32)
    for i in range(n - 1):
        entry_f = jnp.where(i < me, entry_f * decay_len + box[0, i].astype(f32), entry_f)
    entry_b = jnp.zeros((16, width), f32)
    for i in reversed(range(1, n)):
        entry_b = jnp.where(i > me, entry_b * decay_len + box[0, i].astype(f32), entry_b)
    blocks_f, blocks_b = block_rows(entry_f), block_rows(entry_b)
    for j in range(chunks):
        rows = pl.ds(j * L, L)
        ahead = jnp.exp(-float(j * L) * rate_row)
        behind = jnp.exp(-float(length - L - j * L) * rate_row)
        conv = conv_s[rows, :] + outer(split(head * ahead), blocks_f)
        grad = grad_s[rows, :] + outer(split(tail * behind), blocks_b)
        mixed_ref[rows, :] = (q_s[rows, :].astype(f32) * conv).astype(bf16)
        qgrad_ref[rows, :] = (c_s[rows, :].astype(f32) * conv).astype(bf16)
        kgrad_ref[rows, :] = (grad * v_s[rows, :].astype(f32)).astype(bf16)
        vgrad_ref[rows, :] = (grad * k_s[rows, :].astype(f32)).astype(bf16)

    for peer in ids:
        arrived(1, peer).wait_recv()
    for peer in ids:
        pltpu.make_async_remote_copy(
            src_ref=wbox.at[peer],
            dst_ref=wbox.at[peer],
            send_sem=send_sem.at[2, peer],
            recv_sem=recv_sem.at[2, peer],
            device_id={"seq": peer},
            device_id_type=MESH,
        ).wait_recv()
    prefix = jnp.zeros((16, width), f32)
    cross = jnp.zeros((16, width), f32)
    total = wbox[0]
    for i in range(1, n):
        last = jnp.where(i - 1 < me, box[0, i - 1], box[1, i - 1])
        here = jnp.where(i < me, box[1, i], box[0, i])
        prefix = prefix * decay_len + last.astype(f32)
        cross = cross + prefix * here.astype(f32)
        total = total + wbox[i]
    total = (total + group_row(cross * decay_one)) * factor_row
    rgrad_ref[...] = dot(total * in_group, in_mode, ((1,), (1,)), HIGH)
    for copy in sends:
        copy.wait_send()


def writer(*refs):
    count = len(refs) // 2
    sources, targets, sem = refs[:count], refs[count : 2 * count], refs[-1]
    copies = [
        pltpu.make_async_copy(src, dst, sem.at[i])
        for i, (src, dst) in enumerate(zip(sources, targets))
    ]
    for copy in copies:
        copy.start()
    for copy in copies:
        copy.wait()


def peer_table():
    offsets = [(a, b) for a in range(2) for b in range(8) if (a, b) != (0, 0)]
    offsets.sort(key=lambda o: -(2 * o[0] + min(o[1], 8 - o[1])))

    def peers(me, i):
        a, b = offsets[i]
        return ((me // 8 + a) % 2) * 8 + (me % 8 + b) % 8

    return peers


def body(query_gate, key_gate, values_in, cotangent, decay_rate, residues):
    length, width = query_gate.shape
    n = lax.axis_size("seq")
    chunks = length // L
    big = (length, width)
    shapes = [pltpu.VMEM(big, bf16)] * 4 + [pltpu.VMEM(residues.shape, f32)]
    vmem = pl.BlockSpec(memory_space=pltpu.VMEM)
    hbm = pl.BlockSpec(memory_space=pltpu.HBM)

    def stay(x):
        return pltpu.with_memory_space_constraint(x, pltpu.HBM)

    results = pl.pallas_call(
        lambda *refs: kernel(peer_table(), *refs),
        out_shape=shapes,
        in_specs=[hbm] * 6,
        out_specs=[vmem] * 5,
        scratch_shapes=[pltpu.VMEM(residues.shape, f32)] * 2
        + [pltpu.VMEM(big, bf16)] * 7
        + [pltpu.VMEM(big, f32)] * 2
        + [pltpu.VMEM((chunks, MODES, width), f32)] * 3
        + [
            pltpu.VMEM((2, n, MODES, width), bf16),
            pltpu.VMEM((n, 1, width), f32),
            pltpu.SemaphoreType.DMA((6,)),
            pltpu.SemaphoreType.DMA((3, n)),
            pltpu.SemaphoreType.DMA((3, n)),
        ],
        compiler_params=pltpu.CompilerParams(
            collective_id=0, has_side_effects=True, vmem_limit_bytes=40 * 2**20
        ),
        name="scan",
    )(*map(stay, (query_gate, key_gate, values_in, cotangent, decay_rate, residues)))
    results = [pltpu.with_memory_space_constraint(r, pltpu.VMEM) for r in results]
    return tuple(
        pl.pallas_call(
            writer,
            out_shape=[jax.ShapeDtypeStruct(r.shape, r.dtype) for r in results],
            in_specs=[vmem] * 5,
            out_specs=[hbm] * 5,
            scratch_shapes=[pltpu.SemaphoreType.DMA((5,))],
            name="write",
        )(*results)
    )


def solution(mesh):
    wide = P("seq", "chan")
    small = P("chan", None)
    return jax.shard_map(
        body,
        mesh=mesh,
        in_specs=(wide,) * 4 + (small,) * 2,
        out_specs=(wide,) * 4 + (small,),
        check_vma=False,
    )
```

```python
import jax
import jax.numpy as jnp
from jax import lax
from jax.experimental import pallas as pl
from jax.experimental.pallas import tpu as pltpu
from jax.sharding import PartitionSpec as P

MESH = pl.DeviceIdType.MESH
f32 = jnp.float32
bf16 = jnp.bfloat16
GROUP = 16
MODES = 16
L = 64
QUARTER = 64
HIGH = lax.Precision.HIGHEST


def dot(a, b, dims=((1,), (0,)), precision=None):
    return lax.dot_general(
        a, b, (dims, ((), ())), precision=precision, preferred_element_type=f32
    )


def split(x):
    hi = x.astype(bf16)
    return hi, (x - hi.astype(f32)).astype(bf16)


def iota(shape, axis):
    return lax.broadcasted_iota(jnp.int32, shape, axis)


def pick_rows(m, rows):
    left = iota((rows, 128), 1) < QUARTER
    return jnp.concatenate(
        [
            jnp.where(left, m[:rows, :128], m[rows : 2 * rows, :128]),
            jnp.where(left, m[2 * rows : 3 * rows, 128:], m[3 * rows :, 128:]),
        ],
        axis=1,
    )


def kernel(
    peers,
    q_hbm, k_hbm, v_hbm, c_hbm, rate_hbm, res_hbm,
    mixed_ref, qgrad_ref, kgrad_ref, vgrad_ref, rgrad_ref,
    small_s, kv_s, cq_s, x_s, sh_s, sl_s, conv_s, grad_s, fwd_s, bwd_s, bend_s,
    rise_s, fall_s, box, wbox, rbox, in_sem, send_sem, recv_sem, ready,
):
    length, width = x_s.shape
    chunks = length // L
    me = lax.axis_index("seq")
    n = lax.axis_size("seq")
    loads = (
        ((rate_hbm, small_s.at[0]), (res_hbm, small_s.at[1])),
        ((k_hbm, kv_s.at[0]), (v_hbm, kv_s.at[1])),
        ((c_hbm, cq_s.at[0]), (q_hbm, cq_s.at[1])),
    )
    for i, pair in enumerate(loads):
        for src, dst in pair:
            pltpu.make_async_copy(src, dst, in_sem.at[i]).start()

    def loaded(i):
        both = (small_s, kv_s, cq_s)[i]
        pltpu.make_async_copy(both, both, in_sem.at[i]).wait()

    k_s, v_s, c_s, q_s = kv_s.at[0], kv_s.at[1], cq_s.at[0], cq_s.at[1]
    ids = [peers(me, i) for i in range(n - 1)]
    column0 = lax.axis_index("chan") == 0
    first = me == 0
    collector = 1 + column0.astype(jnp.int32)
    middle = jnp.logical_and(me >= 4, me <= 6)
    late = jnp.logical_or(middle, me >= 10)
    late = jnp.logical_or(late, jnp.logical_and(column0, first))
    barrier = pltpu.get_barrier_semaphore()

    @pl.when(jnp.logical_not(jnp.logical_and(column0, first)))
    def _():
        for peer in ids:
            pl.semaphore_signal(
                barrier, inc=1, device_id={"seq": peer}, device_id_type=MESH
            )

    loaded(0)
    rate = small_s[0]
    factor = jnp.sqrt(1.0 - jnp.exp(-2.0 * rate))
    scaled = small_s[1] * factor
    lane_hi = iota((16, width), 1) // GROUP
    lane_lo = iota((16, width), 1) % GROUP
    row16 = iota((16, width), 0)
    in_group = (lane_hi == row16).astype(f32)
    in_mode = (lane_lo == row16).astype(f32)

    def thirds(x):
        hi, rest = x.astype(bf16), x - x.astype(bf16).astype(f32)
        mid, low = split(rest)
        return jnp.concatenate([hi, mid, low], axis=0)

    lane = iota((16, width), 1)
    picks = [row16 == quarter * 4 + lane // L for quarter in range(4)]
    picks = jnp.concatenate(picks + [lane_hi == row16], axis=1).astype(bf16)
    rates = dot(thirds(rate), jnp.concatenate([picks] * 3, axis=0), ((0,), (0,)))
    rate_mc = rates[:, 4 * width :]

    position = (lane % L).astype(f32)
    end_parts = []
    start_parts = []
    for quarter in range(4):
        here = rates[:, quarter * width : (quarter + 1) * width]
        end_parts.append(jnp.exp((position - (L - 1.0)) * here))
        start_parts.append(jnp.exp(-position * here))
    end_hi, end_lo = zip(*[split(x) for x in end_parts])
    start_hi, start_lo = zip(*[split(x) for x in start_parts])

    def halves(hi, lo):
        return [
            jnp.concatenate([hi[2 * h], hi[2 * h + 1], lo[2 * h], lo[2 * h + 1]], axis=0)
            for h in range(2)
        ]

    end_pow = halves(end_hi, end_lo)
    start_pow = halves(start_hi, start_lo)

    lane64 = iota((L, width), 1)
    mask_i = [((lane64 // GROUP) % 4 == i).astype(bf16) for i in range(4)]
    mask_q = [(lane64 // QUARTER == q).astype(bf16) for q in range(4)]

    def spread_i(x):
        return jnp.concatenate([x * m for m in mask_i], axis=0)

    left16 = iota((16, 128), 1) < QUARTER

    def state_of(tables, pieces):
        out = []
        for h in range(2):
            first, *rest = pieces
            r = dot(tables[h], first[:, 128 * h : 128 * h + 128])
            r = r[:32] + r[32:]
            for piece in rest:
                r = r + dot(tables[h][:32], piece[:, 128 * h : 128 * h + 128])
            out.append(jnp.where(left16, r[:16], r[16:]))
        return jnp.concatenate(out, axis=1)

    decay_chunk = jnp.exp(-float(L) * rate_mc)
    decay_len = jnp.exp(-float(length) * rate_mc)
    decay_one = jnp.exp(-rate_mc)

    loaded(1)
    state = jnp.zeros((16, width), f32)
    for j in range(chunks):
        rows = pl.ds(j * L, L)
        x = (k_s[rows, :].astype(f32) * v_s[rows, :].astype(f32)).astype(bf16)
        x_s[rows, :] = x
        fwd_s[j] = state
        state = state * decay_chunk + state_of(end_pow, [spread_i(x)])
    end_state = state.astype(bf16)

    loaded(2)
    state = jnp.zeros((16, width), f32)
    for j in reversed(range(chunks)):
        rows = pl.ds(j * L, L)
        hi, lo = split(c_s[rows, :].astype(f32) * q_s[rows, :].astype(f32))
        sh_s[rows, :] = hi
        sl_s[rows, :] = lo
        bwd_s[j] = state
        here = state_of(start_pow, [spread_i(hi), spread_i(lo)])
        bend_s[j] = here
        state = state * decay_chunk + here
    box[0, me] = state.astype(bf16)
    box[1, me] = end_state

    def row_of(x):
        return jnp.sum(dot(x, in_mode, precision=HIGH) * in_group, axis=0, keepdims=True)

    rate_row, scaled_row, factor_row = row_of(rate), row_of(scaled), row_of(factor)
    row_at, col_at = iota((width, width), 0) % L, iota((width, width), 1) % L
    causal = row_at >= col_at
    wide_lane = iota((width, width), 1)
    wide_row = iota((width, width), 0)
    same_group = ((wide_row // GROUP) == (wide_lane // GROUP)).astype(bf16)

    def group_row(z):
        hi, rest = z.astype(bf16), z - z.astype(bf16).astype(f32)
        mid, low = split(rest)
        s = dot(jnp.concatenate([hi, mid, low], axis=0), same_group)
        s = s[:16] + s[16:32] + s[32:]
        return jnp.sum(s * in_mode, axis=0, keepdims=True)


    step = iota((L, width), 0).astype(f32)
    fall = jnp.exp(-step * rate_row)
    rise = jnp.exp(step * rate_row)
    q_of = iota((L, width), 1) // QUARTER

    def by_quarter(x):
        return jnp.concatenate([jnp.where(q_of == q, x, 0.0) for q in range(4)], axis=0)

    def column(x):
        wide = dot(in_group, x, ((0,), (0,)), HIGH)
        keep = iota((width, MODES), 0) % MODES == iota((width, MODES), 1)
        ones = jnp.ones((MODES, width), f32)
        return dot(jnp.where(keep, wide, 0.0), ones, precision=HIGH)

    same_i = (wide_row // MODES) % 4 == wide_lane // L
    at = (wide_lane % L).astype(f32)

    def product(a, b):
        a_hi, a_lo = split(a)
        b_hi, b_lo = split(b)
        return dot(a_hi, b_hi) + (dot(a_lo, b_hi) + dot(a_hi, b_lo))

    def residue_part():
        rise_cols = jnp.where(same_i, jnp.exp(at * column(rate)), 0.0)
        fall_rows = by_quarter(fall)
        rise_s[...] = rise_cols
        fall_s[...] = fall_rows
        gram = jnp.zeros((width, width), f32)
        cross = jnp.zeros((16, width), f32)
        for j in range(chunks):
            rows = pl.ds(j * L, L)
            hi = sh_s[rows, :]
            lhs = jnp.concatenate([hi * m for m in mask_q], axis=0)
            gram = gram + dot(lhs, spread_i(x_s[rows, :]), ((1,), (1,)))
            cross = cross + fwd_s[j] * bend_s[j]
        gram = jnp.where(causal, gram, 0.0)
        g_hi, g_lo = split(gram)
        r_hi = rise_cols.astype(bf16)
        within = dot(g_hi, r_hi, ((1,), (1,))) + dot(g_lo, r_hi, ((1,), (1,)))
        within = jnp.sum(within * fall_rows, axis=0, keepdims=True)
        wbox[me] = within + group_row(cross * decay_one)

    def block_rows(x):
        hi, lo = split(x)
        masks = [in_group[g : g + 1, :].astype(bf16) for g in range(16)]
        return (
            jnp.concatenate([hi * m for m in masks], axis=0),
            jnp.concatenate([lo * m for m in masks], axis=0),
        )

    def outer(table, blocks):
        t_hi, t_lo = table
        b_hi, b_lo = blocks
        return dot(t_hi, b_hi) + (dot(t_lo, b_hi) + dot(t_hi, b_lo))

    head = fall * jnp.exp(-rate_row) * scaled_row
    tail = rise * jnp.exp(-float(L) * rate_row) * scaled_row
    head_t, tail_t = split(head), split(tail)

    def inner_part():
        rate_col, scaled_col = column(rate), column(scaled)
        fall_cols = jnp.where(same_i, scaled_col * jnp.exp(-at * rate_col), 0.0)
        filt = product(fall_s[...] * scaled_row, rise_s[...])
        anti = product(by_quarter(rise), fall_cols)
        filt = jnp.where(causal, filt, 0.0).astype(bf16)
        anti = jnp.where(row_at <= col_at, anti, 0.0).astype(bf16)
        for j in range(chunks):
            rows = pl.ds(j * L, L)
            inner = pick_rows(dot(filt, spread_i(x_s[rows, :])), L)
            conv_s[rows, :] = inner + outer(head_t, block_rows(fwd_s[j]))
            inner = pick_rows(
                dot(anti, spread_i(sh_s[rows, :])) + dot(anti, spread_i(sl_s[rows, :])), L
            )
            grad_s[rows, :] = inner + outer(tail_t, block_rows(bwd_s[j]))


    @pl.when(jnp.logical_not(late))
    def _():
        residue_part()
        inner_part()

    others_in = jnp.where(jnp.logical_and(column0, jnp.logical_not(first)), n - 2, n - 1)
    pl.semaphore_wait(barrier, others_in)

    def send(source, target, kind, peer):
        return pltpu.make_async_remote_copy(
            src_ref=source,
            dst_ref=target,
            send_sem=send_sem.at[kind],
            recv_sem=recv_sem.at[kind],
            device_id={"seq": peer},
            device_id_type=MESH,
        )

    def near(peer):
        later = (peer > me).astype(jnp.int32)
        return send(box.at[later, me], box.at[0, me], 0, peer)

    def far():
        other = (collector < me).astype(jnp.int32)
        return send(box.at[other, me], box.at[1, me], 1, collector)

    def partial_sum():
        return send(wbox.at[me], wbox.at[me], 2, collector)

    def result(peer):
        return send(rbox.at[0], rbox.at[0], 3, peer)

    def all_of(kind):
        some = pl.ds(0, n - 1)
        ref = (box.at[0, some], box.at[1, some], wbox.at[some], rbox.at[some])[kind]
        return send(ref, ref, kind, me)

    is_collector = me == collector

    @pl.when(jnp.logical_and(column0, first))
    def _():
        for peer in ids:
            pl.semaphore_signal(ready, inc=1, device_id={"seq": peer}, device_id_type=MESH)

    for place, peer in enumerate((0, 1, 8, 2, 7, 9, 15, 3, 6, 10, 14, 5, 11, 13, 4, 12)):
        wanted = me != peer
        if peer == 0:
            wanted = jnp.logical_and(wanted, jnp.logical_not(column0))

        @pl.when(wanted)
        def _():
            near(peer).start()

        if place == 3:

            @pl.when(jnp.logical_not(is_collector))
            def _():
                far().start()

    @pl.when(late)
    def _():
        residue_part()

    @pl.when(jnp.logical_not(is_collector))
    def _():
        partial_sum().start()

    @pl.when(late)
    def _():
        inner_part()

    @pl.when(jnp.logical_and(column0, jnp.logical_not(first)))
    def _():
        pl.semaphore_wait(ready, 1)
        near(0).start()

    all_of(0).wait_recv()
    entry_f = jnp.zeros((16, width), f32)
    for i in range(n - 1):
        entry_f = jnp.where(i < me, entry_f * decay_len + box[0, i].astype(f32), entry_f)
    entry_b = jnp.zeros((16, width), f32)
    for i in reversed(range(1, n)):
        entry_b = jnp.where(i > me, entry_b * decay_len + box[0, i].astype(f32), entry_b)

    @pl.when(is_collector)
    def _():
        all_of(1).wait_recv()
        all_of(2).wait_recv()
        prefix = jnp.zeros((16, width), f32)
        cross = jnp.zeros((16, width), f32)
        total = wbox[0]
        for i in range(1, n):
            last = jnp.where(i - 1 < me, box[0, i - 1], box[1, i - 1])
            here = jnp.where(i < me, box[1, i], box[0, i])
            prefix = prefix * decay_len + last.astype(f32)
            cross = cross + prefix * here.astype(f32)
            total = total + wbox[i]
        total = (total + group_row(cross * decay_one)) * factor_row
        rbox[0] = dot(total * in_group, in_mode, ((1,), (1,)), HIGH)
        for peer in ids:
            result(peer).start()

    blocks_f, blocks_b = block_rows(entry_f), block_rows(entry_b)
    for j in range(chunks):
        rows = pl.ds(j * L, L)
        ahead = jnp.exp(-float(j * L) * rate_row)
        behind = jnp.exp(-float(length - L - j * L) * rate_row)
        conv = conv_s[rows, :] + outer(split(head * ahead), blocks_f)
        grad = grad_s[rows, :] + outer(split(tail * behind), blocks_b)
        mixed_ref[rows, :] = (q_s[rows, :].astype(f32) * conv).astype(bf16)
        qgrad_ref[rows, :] = (c_s[rows, :].astype(f32) * conv).astype(bf16)
        kgrad_ref[rows, :] = (grad * v_s[rows, :].astype(f32)).astype(bf16)
        vgrad_ref[rows, :] = (grad * k_s[rows, :].astype(f32)).astype(bf16)


    @pl.when(jnp.logical_not(is_collector))
    def _():
        result(collector).wait_recv()

    rgrad_ref[...] = rbox[0]
    all_of(0).wait_send()

    @pl.when(is_collector)
    def _():
        all_of(3).wait_send()

    @pl.when(jnp.logical_not(is_collector))
    def _():
        far().wait_send()
        partial_sum().wait_send()


def writer(*refs):
    count = len(refs) // 2
    sources, targets, sem = refs[:count], refs[count : 2 * count], refs[-1]
    copies = [
        pltpu.make_async_copy(src, dst, sem.at[i])
        for i, (src, dst) in enumerate(zip(sources, targets))
    ]
    for copy in copies:
        copy.start()
    for copy in copies:
        copy.wait()


def peer_table():
    offsets = [(a, b) for a in range(2) for b in range(8) if (a, b) != (0, 0)]
    offsets.sort(key=lambda o: -(2 * o[0] + min(o[1], 8 - o[1])))

    def peers(me, i):
        a, b = offsets[i]
        return ((me // 8 + a) % 2) * 8 + (me % 8 + b) % 8

    return peers


def body(query_gate, key_gate, values_in, cotangent, decay_rate, residues):
    length, width = query_gate.shape
    n = lax.axis_size("seq")
    chunks = length // L
    big = (length, width)
    shapes = [pltpu.VMEM(big, bf16)] * 4 + [pltpu.VMEM(residues.shape, f32)]
    vmem = pl.BlockSpec(memory_space=pltpu.VMEM)
    hbm = pl.BlockSpec(memory_space=pltpu.HBM)

    def stay(x):
        return pltpu.with_memory_space_constraint(x, pltpu.HBM)

    results = pl.pallas_call(
        lambda *refs: kernel(peer_table(), *refs),
        out_shape=shapes,
        in_specs=[hbm] * 6,
        out_specs=[vmem] * 5,
        scratch_shapes=[pltpu.VMEM((2,) + residues.shape, f32)]
        + [pltpu.VMEM((2,) + big, bf16)] * 2
        + [pltpu.VMEM(big, bf16)] * 3
        + [pltpu.VMEM(big, f32)] * 2
        + [pltpu.VMEM((chunks, MODES, width), f32)] * 3
        + [
            pltpu.VMEM((width, width), f32),
            pltpu.VMEM((width, width), f32),
            pltpu.VMEM((2, n, MODES, width), bf16),
            pltpu.VMEM((n, 1, width), f32),
            pltpu.VMEM((n,) + residues.shape, f32),
            pltpu.SemaphoreType.DMA((3,)),
            pltpu.SemaphoreType.DMA((4,)),
            pltpu.SemaphoreType.DMA((4,)),
            pltpu.SemaphoreType.REGULAR,
        ],
        compiler_params=pltpu.CompilerParams(
            collective_id=0, has_side_effects=True, vmem_limit_bytes=40 * 2**20
        ),
        name="scan",
    )(*map(stay, (query_gate, key_gate, values_in, cotangent, decay_rate, residues)))
    results = [pltpu.with_memory_space_constraint(r, pltpu.VMEM) for r in results]
    return tuple(
        pl.pallas_call(
            writer,
            out_shape=[jax.ShapeDtypeStruct(r.shape, r.dtype) for r in results],
            in_specs=[vmem] * 5,
            out_specs=[hbm] * 5,
            scratch_shapes=[pltpu.SemaphoreType.DMA((5,))],
            name="write",
        )(*results)
    )


def solution(mesh):
    wide = P("seq", "chan")
    small = P("chan", None)
    return jax.shard_map(
        body,
        mesh=mesh,
        in_specs=(wide,) * 4 + (small,) * 2,
        out_specs=(wide,) * 4 + (small,),
        check_vma=False,
    )
```

```python
import jax
import jax.numpy as jnp
from jax import lax
from jax.experimental import pallas as pl
from jax.experimental.pallas import tpu as pltpu
from jax.sharding import PartitionSpec as P

MESH = pl.DeviceIdType.MESH
f32 = jnp.float32
bf16 = jnp.bfloat16
GROUP = 16
MODES = 16
L = 64
QUARTER = 64
HIGH = lax.Precision.HIGHEST


def dot(a, b, dims=((1,), (0,)), precision=None):
    return lax.dot_general(
        a, b, (dims, ((), ())), precision=precision, preferred_element_type=f32
    )


def split(x):
    hi = x.astype(bf16)
    return hi, (x - hi.astype(f32)).astype(bf16)


def iota(shape, axis):
    return lax.broadcasted_iota(jnp.int32, shape, axis)


def pick_rows(m, rows):
    left = iota((rows, 128), 1) < QUARTER
    return jnp.concatenate(
        [
            jnp.where(left, m[:rows, :128], m[rows : 2 * rows, :128]),
            jnp.where(left, m[2 * rows : 3 * rows, 128:], m[3 * rows :, 128:]),
        ],
        axis=1,
    )


def kernel(
    peers,
    q_hbm, k_hbm, v_hbm, c_hbm, rate_hbm, res_hbm,
    mixed_ref, qgrad_ref, kgrad_ref, vgrad_ref, rrow_ref,
    small_s, kv_s, cq_s, x_s, sh_s, sl_s, conv_s, grad_s, fwd_s, bwd_s, bend_s,
    rise_s, fall_s, head_s, tail_s, box, wbox, rbox, in_sem, send_sem, recv_sem, ready,
):
    length, width = x_s.shape
    chunks = length // L
    me = lax.axis_index("seq")
    n = lax.axis_size("seq")
    loads = (
        ((rate_hbm, small_s.at[0]), (res_hbm, small_s.at[1])),
        ((k_hbm, kv_s.at[0]), (v_hbm, kv_s.at[1])),
        ((c_hbm, cq_s.at[0]), (q_hbm, cq_s.at[1])),
    )
    for i, pair in enumerate(loads):
        for src, dst in pair:
            pltpu.make_async_copy(src, dst, in_sem.at[i]).start()

    def loaded(i):
        both = (small_s, kv_s, cq_s)[i]
        pltpu.make_async_copy(both, both, in_sem.at[i]).wait()

    k_s, v_s, c_s, q_s = kv_s.at[0], kv_s.at[1], cq_s.at[0], cq_s.at[1]
    ids = [peers(me, i) for i in range(n - 1)]
    column0 = lax.axis_index("chan") == 0
    first = me == 0
    per = n // 2
    place = lax.rem(me, per)
    collectors = [column0.astype(jnp.int32), per]
    own_half = me - place
    is_collector = jnp.logical_or(me == collectors[0], me == collectors[1])
    late = jnp.logical_and(me >= 3, me != 8)
    late = jnp.logical_or(late, jnp.logical_and(column0, first))
    last = jnp.logical_and(me >= 12, me <= 14)
    last = jnp.logical_or(last, jnp.logical_and(column0, first))
    barrier = pltpu.get_barrier_semaphore()

    @pl.when(jnp.logical_not(jnp.logical_and(column0, first)))
    def _():
        for peer in ids:
            pl.semaphore_signal(
                barrier, inc=1, device_id={"seq": peer}, device_id_type=MESH
            )

    loaded(0)
    rate = small_s[0]
    factor = jnp.sqrt(1.0 - jnp.exp(-2.0 * rate))
    scaled = small_s[1] * factor
    lane_hi = iota((16, width), 1) // GROUP
    lane_lo = iota((16, width), 1) % GROUP
    row16 = iota((16, width), 0)
    in_group = (lane_hi == row16).astype(f32)
    in_mode = (lane_lo == row16).astype(f32)

    def thirds(x):
        hi, rest = x.astype(bf16), x - x.astype(bf16).astype(f32)
        mid, low = split(rest)
        return jnp.concatenate([hi, mid, low], axis=0)

    lane = iota((16, width), 1)
    picks = [row16 == quarter * 4 + lane // L for quarter in range(4)]
    picks = jnp.concatenate(picks + [lane_hi == row16], axis=1).astype(bf16)
    rates = dot(thirds(rate), jnp.concatenate([picks] * 3, axis=0), ((0,), (0,)))
    rate_mc = rates[:, 4 * width :]

    position = (lane % L).astype(f32)
    end_parts = []
    start_parts = []
    for quarter in range(4):
        here = rates[:, quarter * width : (quarter + 1) * width]
        end_parts.append(jnp.exp((position - (L - 1.0)) * here))
        start_parts.append(jnp.exp(-position * here))
    end_hi, end_lo = zip(*[split(x) for x in end_parts])
    start_hi, start_lo = zip(*[split(x) for x in start_parts])

    def halves(hi, lo):
        return [
            jnp.concatenate([hi[2 * h], hi[2 * h + 1], lo[2 * h], lo[2 * h + 1]], axis=0)
            for h in range(2)
        ]

    end_pow = halves(end_hi, end_lo)
    start_pow = halves(start_hi, start_lo)

    lane64 = iota((L, width), 1)
    mask_i = [((lane64 // GROUP) % 4 == i).astype(bf16) for i in range(4)]
    mask_q = [(lane64 // QUARTER == q).astype(bf16) for q in range(4)]

    def spread_i(x):
        return jnp.concatenate([x * m for m in mask_i], axis=0)

    left16 = iota((16, 128), 1) < QUARTER

    def state_of(tables, pieces):
        out = []
        for h in range(2):
            first, *rest = pieces
            r = dot(tables[h], first[:, 128 * h : 128 * h + 128])
            r = r[:32] + r[32:]
            for piece in rest:
                r = r + dot(tables[h][:32], piece[:, 128 * h : 128 * h + 128])
            out.append(jnp.where(left16, r[:16], r[16:]))
        return jnp.concatenate(out, axis=1)

    decay_chunk = jnp.exp(-float(L) * rate_mc)
    decay_len = jnp.exp(-float(length) * rate_mc)
    decay_one = jnp.exp(-rate_mc)

    loaded(1)
    state = jnp.zeros((16, width), f32)
    for j in range(chunks):
        rows = pl.ds(j * L, L)
        x = (k_s[rows, :].astype(f32) * v_s[rows, :].astype(f32)).astype(bf16)
        x_s[rows, :] = x
        fwd_s[j] = state
        state = state * decay_chunk + state_of(end_pow, [spread_i(x)])
    end_state = state.astype(bf16)

    loaded(2)
    state = jnp.zeros((16, width), f32)
    for j in reversed(range(chunks)):
        rows = pl.ds(j * L, L)
        hi, lo = split(c_s[rows, :].astype(f32) * q_s[rows, :].astype(f32))
        sh_s[rows, :] = hi
        sl_s[rows, :] = lo
        bwd_s[j] = state
        here = state_of(start_pow, [spread_i(hi), spread_i(lo)])
        bend_s[j] = here
        state = state * decay_chunk + here
    box[0, me] = state.astype(bf16)
    box[1, me] = end_state

    def row_of(x):
        return jnp.sum(dot(x, in_mode, precision=HIGH) * in_group, axis=0, keepdims=True)

    rate_row, scaled_row, factor_row = row_of(rate), row_of(scaled), row_of(factor)
    row_at, col_at = iota((width, width), 0) % L, iota((width, width), 1) % L
    causal = row_at >= col_at
    wide_lane = iota((width, width), 1)
    wide_row = iota((width, width), 0)
    same_group = ((wide_row // GROUP) == (wide_lane // GROUP)).astype(bf16)

    def group_row(z):
        hi, rest = z.astype(bf16), z - z.astype(bf16).astype(f32)
        mid, low = split(rest)
        s = dot(jnp.concatenate([hi, mid, low], axis=0), same_group)
        s = s[:16] + s[16:32] + s[32:]
        return jnp.sum(s * in_mode, axis=0, keepdims=True)


    step = iota((L, width), 0).astype(f32)
    fall = jnp.exp(-step * rate_row)
    rise = jnp.exp(step * rate_row)
    q_of = iota((L, width), 1) // QUARTER

    def by_quarter(x):
        return jnp.concatenate([jnp.where(q_of == q, x, 0.0) for q in range(4)], axis=0)

    def column(x):
        wide = dot(in_group, x, ((0,), (0,)), HIGH)
        keep = iota((width, MODES), 0) % MODES == iota((width, MODES), 1)
        ones = jnp.ones((MODES, width), f32)
        return dot(jnp.where(keep, wide, 0.0), ones, precision=HIGH)

    same_i = (wide_row // MODES) % 4 == wide_lane // L
    at = (wide_lane % L).astype(f32)

    def product(a, b):
        a_hi, a_lo = split(a)
        b_hi, b_lo = split(b)
        return dot(a_hi, b_hi) + (dot(a_lo, b_hi) + dot(a_hi, b_lo))

    def residue_part():
        rise_cols = jnp.where(same_i, jnp.exp(at * column(rate)), 0.0)
        fall_rows = by_quarter(fall)
        rise_s[...] = rise_cols
        fall_s[...] = fall_rows
        gram = jnp.zeros((width, width), f32)
        cross = jnp.zeros((16, width), f32)
        for j in range(chunks):
            rows = pl.ds(j * L, L)
            hi = sh_s[rows, :]
            lhs = jnp.concatenate([hi * m for m in mask_q], axis=0)
            gram = gram + dot(lhs, spread_i(x_s[rows, :]), ((1,), (1,)))
            cross = cross + fwd_s[j] * bend_s[j]
        gram = jnp.where(causal, gram, 0.0)
        g_hi, g_lo = split(gram)
        r_hi = rise_cols.astype(bf16)
        within = dot(g_hi, r_hi, ((1,), (1,))) + dot(g_lo, r_hi, ((1,), (1,)))
        within = jnp.sum(within * fall_rows, axis=0, keepdims=True)
        wbox[me] = within + group_row(cross * decay_one)

    def block_rows(x):
        hi, lo = split(x)
        masks = [in_group[g : g + 1, :].astype(bf16) for g in range(16)]
        return (
            jnp.concatenate([hi * m for m in masks], axis=0),
            jnp.concatenate([lo * m for m in masks], axis=0),
        )

    def outer(table, blocks):
        t_hi, t_lo = table
        b_hi, b_lo = blocks
        return dot(t_hi, b_hi) + (dot(t_lo, b_hi) + dot(t_hi, b_lo))

    head = fall * jnp.exp(-rate_row) * scaled_row
    tail = rise * jnp.exp(-float(L) * rate_row) * scaled_row
    head_t, tail_t = split(head), split(tail)

    def inner_part():
        rate_col, scaled_col = column(rate), column(scaled)
        fall_cols = jnp.where(same_i, scaled_col * jnp.exp(-at * rate_col), 0.0)
        filt = product(fall_s[...] * scaled_row, rise_s[...])
        anti = product(by_quarter(rise), fall_cols)
        filt = jnp.where(causal, filt, 0.0).astype(bf16)
        anti = jnp.where(row_at <= col_at, anti, 0.0).astype(bf16)
        for j in range(chunks):
            rows = pl.ds(j * L, L)
            inner = pick_rows(dot(filt, spread_i(x_s[rows, :])), L)
            conv_s[rows, :] = inner + outer(head_t, block_rows(fwd_s[j]))
            inner = pick_rows(
                dot(anti, spread_i(sh_s[rows, :])) + dot(anti, spread_i(sl_s[rows, :])), L
            )
            grad_s[rows, :] = inner + outer(tail_t, block_rows(bwd_s[j]))
            ahead = jnp.exp(-float(j * L) * rate_row)
            behind = jnp.exp(-float(length - L - j * L) * rate_row)
            head_s[0, rows, :], head_s[1, rows, :] = split(head * ahead)
            tail_s[0, rows, :], tail_s[1, rows, :] = split(tail * behind)


    @pl.when(jnp.logical_not(last))
    def _():
        residue_part()

    @pl.when(jnp.logical_not(late))
    def _():
        inner_part()

    others_in = jnp.where(jnp.logical_and(column0, jnp.logical_not(first)), n - 2, n - 1)
    pl.semaphore_wait(barrier, others_in)

    def send(source, target, kind, peer):
        return pltpu.make_async_remote_copy(
            src_ref=source,
            dst_ref=target,
            send_sem=send_sem.at[kind],
            recv_sem=recv_sem.at[kind],
            device_id={"seq": peer},
            device_id_type=MESH,
        )

    def near(peer):
        later = (peer > me).astype(jnp.int32)
        return send(box.at[later, me], box.at[0, me], 0, peer)

    def far(peer):
        other = (peer < me).astype(jnp.int32)
        return send(box.at[other, me], box.at[1, me], 1, peer)

    def partial_sum(peer):
        return send(wbox.at[me], wbox.at[me], 2, peer)

    def result(peer):
        return send(rbox.at[0], rbox.at[0], 3, peer)

    def all_of(kind, count):
        some = pl.ds(0, count)
        ref = (box.at[0, some], box.at[1, some], wbox.at[some], rbox.at[some])[kind]
        return send(ref, ref, kind, me)

    def to_collectors(fn):
        for peer in collectors:

            @pl.when(me != peer)
            def _():
                fn(peer).start()

    @pl.when(jnp.logical_and(column0, first))
    def _():
        for peer in ids:
            pl.semaphore_signal(ready, inc=1, device_id={"seq": peer}, device_id_type=MESH)

    @pl.when(jnp.logical_not(last))
    def _():
        to_collectors(partial_sum)

    def send_near(peers):
        for peer in peers:
            wanted = me != peer
            if peer == 0:
                wanted = jnp.logical_and(wanted, jnp.logical_not(column0))

            @pl.when(wanted)
            def _():
                near(peer).start()

    send_near((0, 1, 8, 2))
    to_collectors(far)
    send_near((7, 9, 15))

    @pl.when(last)
    def _():
        residue_part()
        to_collectors(partial_sum)

    send_near((3, 6, 10, 14, 5, 11, 13, 4, 12))

    @pl.when(late)
    def _():
        inner_part()

    @pl.when(jnp.logical_and(column0, jnp.logical_not(first)))
    def _():
        pl.semaphore_wait(ready, 1)
        near(0).start()

    all_of(0, n - 1).wait_recv()
    @pl.when(is_collector)
    def _():
        all_of(1, n - 1).wait_recv()
        prefix = jnp.zeros((16, width), f32)
        cross = jnp.zeros((16, width), f32)
        for i in range(1, n):
            last = jnp.where(i - 1 < me, box[0, i - 1], box[1, i - 1])
            here = jnp.where(i < me, box[1, i], box[0, i])
            prefix = prefix * decay_len + last.astype(f32)
            cross = cross + prefix * here.astype(f32)
        total = group_row(cross * decay_one)
        all_of(2, n - 1).wait_recv()
        for i in range(n):
            total = total + wbox[i]
        rbox[0] = total * factor_row
        for peer in (0, 1, 7, 2, 6, 3, 5, 4):

            @pl.when(place != peer)
            def _():
                result(own_half + peer).start()

    entry_f = jnp.zeros((16, width), f32)
    for i in range(n - 1):
        entry_f = jnp.where(i < me, entry_f * decay_len + box[0, i].astype(f32), entry_f)
    entry_b = jnp.zeros((16, width), f32)
    for i in reversed(range(1, n)):
        entry_b = jnp.where(i > me, entry_b * decay_len + box[0, i].astype(f32), entry_b)

    blocks_f, blocks_b = block_rows(entry_f), block_rows(entry_b)

    def lifted(table, rows, blocks):
        hi, lo = table[0, rows, :], table[1, rows, :]
        return dot(hi, blocks[0]) + (dot(lo, blocks[0]) + dot(hi, blocks[1]))

    for j in range(2):
        rows = pl.ds(j * length // 2, length // 2)
        conv = conv_s[rows, :] + lifted(head_s, rows, blocks_f)
        mixed_ref[rows, :] = (q_s[rows, :].astype(f32) * conv).astype(bf16)
        qgrad_ref[rows, :] = (c_s[rows, :].astype(f32) * conv).astype(bf16)
        grad = grad_s[rows, :] + lifted(tail_s, rows, blocks_b)
        kgrad_ref[rows, :] = (grad * v_s[rows, :].astype(f32)).astype(bf16)
        vgrad_ref[rows, :] = (grad * k_s[rows, :].astype(f32)).astype(bf16)

    @pl.when(jnp.logical_not(is_collector))
    def _():
        result(me).wait_recv()

    rrow_ref[...] = rbox[0]
    all_of(0, n - 1).wait_send()

    @pl.when(is_collector)
    def _():
        all_of(3, per - 1).wait_send()
        all_of(1, 1).wait_send()
        all_of(2, 1).wait_send()

    @pl.when(jnp.logical_not(is_collector))
    def _():
        all_of(1, 2).wait_send()
        all_of(2, 2).wait_send()


def writer(*refs):
    *sources, row = refs[:5]
    *targets, residue = refs[5:10]
    small, sem = refs[10:]
    copies = [
        pltpu.make_async_copy(src, dst, sem.at[i])
        for i, (src, dst) in enumerate(zip(sources, targets))
    ]
    for copy in copies:
        copy.start()
    shape = (GROUP, row.shape[1])
    group, lane = iota(shape, 0), iota(shape, 1)
    here = jnp.where(lane // MODES == group, row[...], 0.0)
    mode = (lane % MODES == group).astype(f32)
    small[...] = dot(here, mode, ((1,), (1,)), HIGH)
    copies.append(pltpu.make_async_copy(small, residue, sem.at[4]))
    copies[-1].start()
    for copy in copies:
        copy.wait()


def peer_table():
    offsets = [(a, b) for a in range(2) for b in range(8) if (a, b) != (0, 0)]
    offsets.sort(key=lambda o: -(2 * o[0] + min(o[1], 8 - o[1])))

    def peers(me, i):
        a, b = offsets[i]
        return ((me // 8 + a) % 2) * 8 + (me % 8 + b) % 8

    return peers


def body(query_gate, key_gate, values_in, cotangent, decay_rate, residues):
    length, width = query_gate.shape
    n = lax.axis_size("seq")
    chunks = length // L
    big = (length, width)
    shapes = [pltpu.VMEM(big, bf16)] * 4 + [pltpu.VMEM((1, width), f32)]
    vmem = pl.BlockSpec(memory_space=pltpu.VMEM)
    hbm = pl.BlockSpec(memory_space=pltpu.HBM)

    def stay(x):
        return pltpu.with_memory_space_constraint(x, pltpu.HBM)

    results = pl.pallas_call(
        lambda *refs: kernel(peer_table(), *refs),
        out_shape=shapes,
        in_specs=[hbm] * 6,
        out_specs=[vmem] * 5,
        scratch_shapes=[pltpu.VMEM((2,) + residues.shape, f32)]
        + [pltpu.VMEM((2,) + big, bf16)] * 2
        + [pltpu.VMEM(big, bf16)] * 3
        + [pltpu.VMEM(big, f32)] * 2
        + [pltpu.VMEM((chunks, MODES, width), f32)] * 3
        + [
            pltpu.VMEM((width, width), f32),
            pltpu.VMEM((width, width), f32),
            pltpu.VMEM((2,) + big, bf16),
            pltpu.VMEM((2,) + big, bf16),
            pltpu.VMEM((2, n, MODES, width), bf16),
            pltpu.VMEM((n, 1, width), f32),
            pltpu.VMEM((n, 1, width), f32),
            pltpu.SemaphoreType.DMA((3,)),
            pltpu.SemaphoreType.DMA((4,)),
            pltpu.SemaphoreType.DMA((4,)),
            pltpu.SemaphoreType.REGULAR,
        ],
        compiler_params=pltpu.CompilerParams(
            collective_id=0, has_side_effects=True, vmem_limit_bytes=40 * 2**20
        ),
        name="scan",
    )(*map(stay, (query_gate, key_gate, values_in, cotangent, decay_rate, residues)))
    results = [pltpu.with_memory_space_constraint(r, pltpu.VMEM) for r in results]
    return tuple(
        pl.pallas_call(
            writer,
            out_shape=[jax.ShapeDtypeStruct(big, bf16)] * 4
            + [jax.ShapeDtypeStruct(residues.shape, f32)],
            in_specs=[vmem] * 5,
            out_specs=[hbm] * 5,
            scratch_shapes=[
                pltpu.VMEM(residues.shape, f32),
                pltpu.SemaphoreType.DMA((5,)),
            ],
            name="write",
        )(*results)
    )


def solution(mesh):
    wide = P("seq", "chan")
    small = P("chan", None)
    return jax.shard_map(
        body,
        mesh=mesh,
        in_specs=(wide,) * 4 + (small,) * 2,
        out_specs=(wide,) * 4 + (small,),
        check_vma=False,
    )
```

```python
import jax
import jax.numpy as jnp
from jax import lax
from jax.experimental import pallas as pl
from jax.experimental.pallas import tpu as pltpu
from jax.sharding import PartitionSpec as P

MESH = pl.DeviceIdType.MESH
f32 = jnp.float32
bf16 = jnp.bfloat16
GROUP = 16
MODES = 16
L = 64
QUARTER = 64
HIGH = lax.Precision.HIGHEST


def dot(a, b, dims=((1,), (0,)), precision=None):
    return lax.dot_general(
        a, b, (dims, ((), ())), precision=precision, preferred_element_type=f32
    )


def split(x):
    hi = x.astype(bf16)
    return hi, (x - hi.astype(f32)).astype(bf16)


def iota(shape, axis):
    return lax.broadcasted_iota(jnp.int32, shape, axis)


def pick_rows(m, rows):
    left = iota((rows, 128), 1) < QUARTER
    return jnp.concatenate(
        [
            jnp.where(left, m[:rows, :128], m[rows : 2 * rows, :128]),
            jnp.where(left, m[2 * rows : 3 * rows, 128:], m[3 * rows :, 128:]),
        ],
        axis=1,
    )


def kernel(
    peers,
    q_hbm, k_hbm, v_hbm, c_hbm, rate_hbm, res_hbm,
    mixed_ref, qgrad_ref, kgrad_ref, vgrad_ref, rrow_ref,
    small_s, kv_s, cq_s, x_s, sh_s, sl_s, conv_s, grad_s, fwd_s, bwd_s, bend_s,
    rise_s, fall_s, head_s, tail_s, box, wbox, rbox, in_sem, send_sem, recv_sem, ready,
):
    length, width = x_s.shape
    chunks = length // L
    me = lax.axis_index("seq")
    n = lax.axis_size("seq")
    loads = (
        ((rate_hbm, small_s.at[0]), (res_hbm, small_s.at[1])),
        ((k_hbm, kv_s.at[0]), (v_hbm, kv_s.at[1])),
        ((c_hbm, cq_s.at[0]), (q_hbm, cq_s.at[1])),
    )
    for i, pair in enumerate(loads):
        for src, dst in pair:
            pltpu.make_async_copy(src, dst, in_sem.at[i]).start()

    def loaded(i):
        both = (small_s, kv_s, cq_s)[i]
        pltpu.make_async_copy(both, both, in_sem.at[i]).wait()

    k_s, v_s, c_s, q_s = kv_s.at[0], kv_s.at[1], cq_s.at[0], cq_s.at[1]
    ids = [peers(me, i) for i in range(n - 1)]
    column0 = lax.axis_index("chan") == 0
    first = me == 0
    per = n // 2
    place = lax.rem(me, per)
    collectors = [column0.astype(jnp.int32), per]
    own_half = me - place
    is_collector = jnp.logical_or(me == collectors[0], me == collectors[1])
    late = jnp.logical_and(me >= 3, me != 8)
    late = jnp.logical_or(late, jnp.logical_and(column0, first))
    last = jnp.logical_and(me >= 12, me <= 14)
    last = jnp.logical_or(last, jnp.logical_and(column0, first))
    barrier = pltpu.get_barrier_semaphore()

    @pl.when(jnp.logical_not(jnp.logical_and(column0, first)))
    def _():
        for peer in ids:
            pl.semaphore_signal(
                barrier, inc=1, device_id={"seq": peer}, device_id_type=MESH
            )

    loaded(0)
    rate = small_s[0]
    factor = jnp.sqrt(1.0 - jnp.exp(-2.0 * rate))
    scaled = small_s[1] * factor
    lane_hi = iota((16, width), 1) // GROUP
    lane_lo = iota((16, width), 1) % GROUP
    row16 = iota((16, width), 0)
    in_group = (lane_hi == row16).astype(f32)
    in_mode = (lane_lo == row16).astype(f32)

    def thirds(x):
        hi, rest = x.astype(bf16), x - x.astype(bf16).astype(f32)
        mid, low = split(rest)
        return jnp.concatenate([hi, mid, low], axis=0)

    lane = iota((16, width), 1)
    picks = [row16 == quarter * 4 + lane // L for quarter in range(4)]
    picks = jnp.concatenate(picks + [lane_hi == row16], axis=1).astype(bf16)
    rates = dot(thirds(rate), jnp.concatenate([picks] * 3, axis=0), ((0,), (0,)))
    rate_mc = rates[:, 4 * width :]

    position = (lane % L).astype(f32)
    end_parts = []
    start_parts = []
    for quarter in range(4):
        here = rates[:, quarter * width : (quarter + 1) * width]
        end_parts.append(jnp.exp((position - (L - 1.0)) * here))
        start_parts.append(jnp.exp(-position * here))
    end_hi, end_lo = zip(*[split(x) for x in end_parts])
    start_hi, start_lo = zip(*[split(x) for x in start_parts])

    def halves(hi, lo):
        return [
            jnp.concatenate([hi[2 * h], hi[2 * h + 1], lo[2 * h], lo[2 * h + 1]], axis=0)
            for h in range(2)
        ]

    end_pow = halves(end_hi, end_lo)
    start_pow = halves(start_hi, start_lo)

    lane64 = iota((L, width), 1)
    mask_i = [((lane64 // GROUP) % 4 == i).astype(bf16) for i in range(4)]
    mask_q = [(lane64 // QUARTER == q).astype(bf16) for q in range(4)]

    def spread_i(x):
        return jnp.concatenate([x * m for m in mask_i], axis=0)

    left16 = iota((16, 128), 1) < QUARTER

    def state_of(tables, pieces):
        out = []
        for h in range(2):
            first, *rest = pieces
            r = dot(tables[h], first[:, 128 * h : 128 * h + 128])
            r = r[:32] + r[32:]
            for piece in rest:
                r = r + dot(tables[h][:32], piece[:, 128 * h : 128 * h + 128])
            out.append(jnp.where(left16, r[:16], r[16:]))
        return jnp.concatenate(out, axis=1)

    decay_chunk = jnp.exp(-float(L) * rate_mc)
    decay_len = jnp.exp(-float(length) * rate_mc)
    decay_one = jnp.exp(-rate_mc)

    loaded(1)
    state = jnp.zeros((16, width), f32)
    for j in range(chunks):
        rows = pl.ds(j * L, L)
        x = (k_s[rows, :].astype(f32) * v_s[rows, :].astype(f32)).astype(bf16)
        x_s[rows, :] = x
        fwd_s[j] = state
        state = state * decay_chunk + state_of(end_pow, [spread_i(x)])
    end_state = state.astype(bf16)

    loaded(2)
    state = jnp.zeros((16, width), f32)
    for j in reversed(range(chunks)):
        rows = pl.ds(j * L, L)
        hi, lo = split(c_s[rows, :].astype(f32) * q_s[rows, :].astype(f32))
        sh_s[rows, :] = hi
        sl_s[rows, :] = lo
        bwd_s[j] = state
        here = state_of(start_pow, [spread_i(hi), spread_i(lo)])
        bend_s[j] = here
        state = state * decay_chunk + here
    box[0, me] = state.astype(bf16)
    box[1, me] = end_state

    def row_of(x):
        return jnp.sum(dot(x, in_mode, precision=HIGH) * in_group, axis=0, keepdims=True)

    rate_row, scaled_row, factor_row = row_of(rate), row_of(scaled), row_of(factor)
    row_at, col_at = iota((width, width), 0) % L, iota((width, width), 1) % L
    causal = row_at >= col_at
    wide_lane = iota((width, width), 1)
    wide_row = iota((width, width), 0)
    same_group = ((wide_row // GROUP) == (wide_lane // GROUP)).astype(bf16)

    def group_row(z):
        hi, rest = z.astype(bf16), z - z.astype(bf16).astype(f32)
        mid, low = split(rest)
        s = dot(jnp.concatenate([hi, mid, low], axis=0), same_group)
        s = s[:16] + s[16:32] + s[32:]
        return jnp.sum(s * in_mode, axis=0, keepdims=True)


    step = iota((L, width), 0).astype(f32)
    fall = jnp.exp(-step * rate_row)
    rise = jnp.exp(step * rate_row)
    q_of = iota((L, width), 1) // QUARTER

    def by_quarter(x):
        return jnp.concatenate([jnp.where(q_of == q, x, 0.0) for q in range(4)], axis=0)

    def column(x):
        wide = dot(in_group, x, ((0,), (0,)), HIGH)
        keep = iota((width, MODES), 0) % MODES == iota((width, MODES), 1)
        ones = jnp.ones((MODES, width), f32)
        return dot(jnp.where(keep, wide, 0.0), ones, precision=HIGH)

    same_i = (wide_row // MODES) % 4 == wide_lane // L
    at = (wide_lane % L).astype(f32)

    def product(a, b):
        a_hi, a_lo = split(a)
        b_hi, b_lo = split(b)
        return dot(a_hi, b_hi) + (dot(a_lo, b_hi) + dot(a_hi, b_lo))

    def residue_part():
        rise_cols = jnp.where(same_i, jnp.exp(at * column(rate)), 0.0)
        fall_rows = by_quarter(fall)
        rise_s[...] = rise_cols
        fall_s[...] = fall_rows
        gram = jnp.zeros((width, width), f32)
        cross = jnp.zeros((16, width), f32)
        for j in range(chunks):
            rows = pl.ds(j * L, L)
            hi = sh_s[rows, :]
            lhs = jnp.concatenate([hi * m for m in mask_q], axis=0)
            gram = gram + dot(lhs, spread_i(x_s[rows, :]), ((1,), (1,)))
            cross = cross + fwd_s[j] * bend_s[j]
        gram = jnp.where(causal, gram, 0.0)
        g_hi, g_lo = split(gram)
        r_hi = rise_cols.astype(bf16)
        within = dot(g_hi, r_hi, ((1,), (1,))) + dot(g_lo, r_hi, ((1,), (1,)))
        within = jnp.sum(within * fall_rows, axis=0, keepdims=True)
        wbox[me] = within + group_row(cross * decay_one)

    def block_rows(x):
        hi, lo = split(x)
        masks = [in_group[g : g + 1, :].astype(bf16) for g in range(16)]
        return (
            jnp.concatenate([hi * m for m in masks], axis=0),
            jnp.concatenate([lo * m for m in masks], axis=0),
        )

    def outer(table, blocks):
        t_hi, t_lo = table
        b_hi, b_lo = blocks
        return dot(t_hi, b_hi) + (dot(t_lo, b_hi) + dot(t_hi, b_lo))

    head = fall * jnp.exp(-rate_row) * scaled_row
    tail = rise * jnp.exp(-float(L) * rate_row) * scaled_row
    head_t, tail_t = split(head), split(tail)

    def inner_part():
        rate_col, scaled_col = column(rate), column(scaled)
        fall_cols = jnp.where(same_i, scaled_col * jnp.exp(-at * rate_col), 0.0)
        filt = product(fall_s[...] * scaled_row, rise_s[...])
        anti = product(by_quarter(rise), fall_cols)
        filt = jnp.where(causal, filt, 0.0).astype(bf16)
        anti = jnp.where(row_at <= col_at, anti, 0.0).astype(bf16)
        for j in range(chunks):
            rows = pl.ds(j * L, L)
            inner = pick_rows(dot(filt, spread_i(x_s[rows, :])), L)
            conv_s[rows, :] = inner + outer(head_t, block_rows(fwd_s[j]))
            inner = pick_rows(
                dot(anti, spread_i(sh_s[rows, :])) + dot(anti, spread_i(sl_s[rows, :])), L
            )
            grad_s[rows, :] = inner + outer(tail_t, block_rows(bwd_s[j]))
            ahead = jnp.exp(-float(j * L) * rate_row)
            behind = jnp.exp(-float(length - L - j * L) * rate_row)
            head_s[0, rows, :], head_s[1, rows, :] = split(head * ahead)
            tail_s[0, rows, :], tail_s[1, rows, :] = split(tail * behind)


    @pl.when(jnp.logical_not(last))
    def _():
        residue_part()

    @pl.when(jnp.logical_not(late))
    def _():
        inner_part()

    others_in = jnp.where(jnp.logical_and(column0, jnp.logical_not(first)), n - 2, n - 1)
    pl.semaphore_wait(barrier, others_in)

    def send(source, target, kind, peer):
        return pltpu.make_async_remote_copy(
            src_ref=source,
            dst_ref=target,
            send_sem=send_sem.at[kind],
            recv_sem=recv_sem.at[kind],
            device_id={"seq": peer},
            device_id_type=MESH,
        )

    def near(peer):
        later = (peer > me).astype(jnp.int32)
        return send(box.at[later, me], box.at[0, me], 0, peer)

    def far(peer):
        other = (peer < me).astype(jnp.int32)
        return send(box.at[other, me], box.at[1, me], 1, peer)

    def partial_sum(peer):
        return send(wbox.at[me], wbox.at[me], 2, peer)

    def result(peer):
        return send(rbox.at[0], rbox.at[0], 3, peer)

    def all_of(kind, count):
        some = pl.ds(0, count)
        ref = (box.at[0, some], box.at[1, some], wbox.at[some], rbox.at[some])[kind]
        return send(ref, ref, kind, me)

    def to_collectors(fn):
        for peer in collectors:

            @pl.when(me != peer)
            def _():
                fn(peer).start()

    @pl.when(jnp.logical_and(column0, first))
    def _():
        for peer in ids:
            pl.semaphore_signal(ready, inc=1, device_id={"seq": peer}, device_id_type=MESH)

    @pl.when(jnp.logical_not(last))
    def _():
        to_collectors(partial_sum)

    def send_near(peers):
        for peer in peers:
            wanted = me != peer
            if peer == 0:
                wanted = jnp.logical_and(wanted, jnp.logical_not(column0))

            @pl.when(wanted)
            def _():
                near(peer).start()

    to_collectors(far)
    send_near((0, 1, 8, 2, 7, 9, 15))

    @pl.when(last)
    def _():
        residue_part()
        to_collectors(partial_sum)

    send_near((3, 6, 10, 14, 5, 11, 13, 4, 12))

    @pl.when(late)
    def _():
        inner_part()

    @pl.when(jnp.logical_and(column0, jnp.logical_not(first)))
    def _():
        pl.semaphore_wait(ready, 1)
        near(0).start()

    all_of(0, n - 1).wait_recv()
    @pl.when(is_collector)
    def _():
        all_of(1, n - 1).wait_recv()
        prefix = jnp.zeros((16, width), f32)
        cross = jnp.zeros((16, width), f32)
        for i in range(1, n):
            last = jnp.where(i - 1 < me, box[0, i - 1], box[1, i - 1])
            here = jnp.where(i < me, box[1, i], box[0, i])
            prefix = prefix * decay_len + last.astype(f32)
            cross = cross + prefix * here.astype(f32)
        total = group_row(cross * decay_one)
        all_of(2, n - 1).wait_recv()
        for i in range(n):
            total = total + wbox[i]
        rbox[0] = total * factor_row
        for peer in (0, 1, 7, 2, 6, 3, 5, 4):

            @pl.when(place != peer)
            def _():
                result(own_half + peer).start()

    entry_f = jnp.zeros((16, width), f32)
    for i in range(n - 1):
        entry_f = jnp.where(i < me, entry_f * decay_len + box[0, i].astype(f32), entry_f)
    entry_b = jnp.zeros((16, width), f32)
    for i in reversed(range(1, n)):
        entry_b = jnp.where(i > me, entry_b * decay_len + box[0, i].astype(f32), entry_b)

    blocks_f, blocks_b = block_rows(entry_f), block_rows(entry_b)

    def lifted(table, rows, blocks):
        hi, lo = table[0, rows, :], table[1, rows, :]
        return dot(hi, blocks[0]) + (dot(lo, blocks[0]) + dot(hi, blocks[1]))

    for j in range(2):
        rows = pl.ds(j * length // 2, length // 2)
        conv = conv_s[rows, :] + lifted(head_s, rows, blocks_f)
        mixed_ref[rows, :] = (q_s[rows, :].astype(f32) * conv).astype(bf16)
        qgrad_ref[rows, :] = (c_s[rows, :].astype(f32) * conv).astype(bf16)
        grad = grad_s[rows, :] + lifted(tail_s, rows, blocks_b)
        kgrad_ref[rows, :] = (grad * v_s[rows, :].astype(f32)).astype(bf16)
        vgrad_ref[rows, :] = (grad * k_s[rows, :].astype(f32)).astype(bf16)

    @pl.when(jnp.logical_not(is_collector))
    def _():
        result(me).wait_recv()

    rrow_ref[...] = rbox[0]
    all_of(0, n - 1).wait_send()

    @pl.when(is_collector)
    def _():
        all_of(3, per - 1).wait_send()
        all_of(1, 1).wait_send()
        all_of(2, 1).wait_send()

    @pl.when(jnp.logical_not(is_collector))
    def _():
        all_of(1, 2).wait_send()
        all_of(2, 2).wait_send()


def writer(*refs):
    *sources, row = refs[:5]
    *targets, residue = refs[5:10]
    small, sem = refs[10:]
    copies = [
        pltpu.make_async_copy(src, dst, sem.at[i])
        for i, (src, dst) in enumerate(zip(sources, targets))
    ]
    for copy in copies:
        copy.start()
    shape = (GROUP, row.shape[1])
    group, lane = iota(shape, 0), iota(shape, 1)
    here = jnp.where(lane // MODES == group, row[...], 0.0)
    mode = (lane % MODES == group).astype(f32)
    small[...] = dot(here, mode, ((1,), (1,)), HIGH)
    copies.append(pltpu.make_async_copy(small, residue, sem.at[4]))
    copies[-1].start()
    for copy in copies:
        copy.wait()


def peer_table():
    offsets = [(a, b) for a in range(2) for b in range(8) if (a, b) != (0, 0)]
    offsets.sort(key=lambda o: -(2 * o[0] + min(o[1], 8 - o[1])))

    def peers(me, i):
        a, b = offsets[i]
        return ((me // 8 + a) % 2) * 8 + (me % 8 + b) % 8

    return peers


def body(query_gate, key_gate, values_in, cotangent, decay_rate, residues):
    length, width = query_gate.shape
    n = lax.axis_size("seq")
    chunks = length // L
    big = (length, width)
    shapes = [pltpu.VMEM(big, bf16)] * 4 + [pltpu.VMEM((1, width), f32)]
    vmem = pl.BlockSpec(memory_space=pltpu.VMEM)
    hbm = pl.BlockSpec(memory_space=pltpu.HBM)

    def stay(x):
        return pltpu.with_memory_space_constraint(x, pltpu.HBM)

    results = pl.pallas_call(
        lambda *refs: kernel(peer_table(), *refs),
        out_shape=shapes,
        in_specs=[hbm] * 6,
        out_specs=[vmem] * 5,
        scratch_shapes=[pltpu.VMEM((2,) + residues.shape, f32)]
        + [pltpu.VMEM((2,) + big, bf16)] * 2
        + [pltpu.VMEM(big, bf16)] * 3
        + [pltpu.VMEM(big, f32)] * 2
        + [pltpu.VMEM((chunks, MODES, width), f32)] * 3
        + [
            pltpu.VMEM((width, width), f32),
            pltpu.VMEM((width, width), f32),
            pltpu.VMEM((2,) + big, bf16),
            pltpu.VMEM((2,) + big, bf16),
            pltpu.VMEM((2, n, MODES, width), bf16),
            pltpu.VMEM((n, 1, width), f32),
            pltpu.VMEM((n, 1, width), f32),
            pltpu.SemaphoreType.DMA((3,)),
            pltpu.SemaphoreType.DMA((4,)),
            pltpu.SemaphoreType.DMA((4,)),
            pltpu.SemaphoreType.REGULAR,
        ],
        compiler_params=pltpu.CompilerParams(
            collective_id=0, has_side_effects=True, vmem_limit_bytes=40 * 2**20
        ),
        name="scan",
    )(*map(stay, (query_gate, key_gate, values_in, cotangent, decay_rate, residues)))
    results = [pltpu.with_memory_space_constraint(r, pltpu.VMEM) for r in results]
    return tuple(
        pl.pallas_call(
            writer,
            out_shape=[jax.ShapeDtypeStruct(big, bf16)] * 4
            + [jax.ShapeDtypeStruct(residues.shape, f32)],
            in_specs=[vmem] * 5,
            out_specs=[hbm] * 5,
            scratch_shapes=[
                pltpu.VMEM(residues.shape, f32),
                pltpu.SemaphoreType.DMA((5,)),
            ],
            name="write",
        )(*results)
    )


def solution(mesh):
    wide = P("seq", "chan")
    small = P("chan", None)
    return jax.shard_map(
        body,
        mesh=mesh,
        in_specs=(wide,) * 4 + (small,) * 2,
        out_specs=(wide,) * 4 + (small,),
        check_vma=False,
    )
```
